32 devices in a mesh: seq: 16 (over z, x, core), fsdp: 2 (over y).
Axes of the slice: x: 2, y: 2, z: 4, core: 2. Of those that a mesh axis runs over, the one named last changes fastest.
Arguments:
- queries: bfloat16 [8192, 2048], P('seq', 'fsdp'), may hold values from -6 to 6
- keys: bfloat16 [8192, 2048], P('seq', 'fsdp'), may hold values from -6 to 6
- values: bfloat16 [8192, 2048], P('seq', 'fsdp'), may hold values from -6 to 6
- feature_weight: bfloat16 [16, 128, 128], P(None, 'fsdp', 'seq'), may hold values from -0.5 to 0.5
- norm_gain: bfloat16 [16, 128], P('fsdp'), may hold values from 0.099609375 to 1.8984375
- doc_bounds: int32 [4, 2], replicated, may hold values from 0 to 64, as said below
- out_grad: bfloat16 [8192, 2048], P('seq', 'fsdp'), may hold values from -6 to 6
Outputs:
- mixed: bfloat16 [8192, 2048], P('seq', 'fsdp')
- query_grad: bfloat16 [8192, 2048], P('seq', 'fsdp')
- key_grad: bfloat16 [8192, 2048], P('seq', 'fsdp')
- value_grad: bfloat16 [8192, 2048], P('seq', 'fsdp')
- weight_grad: float32 [16, 128, 128], P(None, 'fsdp', 'seq')
- gain_grad: float32 [16, 128], P('fsdp')
The draws below stay inside these ranges and needn't reach their ends.
Inputs may be any that keep to these rules, and one draw needn't show every extreme that they name: `doc_bounds`: the rows list the 4 documents in order: column 0 is the first block and column 1 the block after the last; the first document starts at block 0, each ends where the next starts, the last ends at block 64; every document holds one block or more of 128 tokens.
All inputs are finite; a program needn't handle non-finite values.
Results may differ from the reference program's by a relative error of at most 0.015.
Values may be sent and summed in bfloat16 or wider, within the bound.
A program may use at most 64 MiB of HBM per device.

```python
from functools import partial
import jax
import jax.numpy as jnp
from jax import lax

H = 16
HS = 128
BLK = 128
DOCS = 4
HD = 2048
LEN = 8192
NBLK = 64


def draw_doc_bounds(key, part):
    borders = jax.random.permutation(key, NBLK - 1)[:DOCS - 1] + 1
    borders = jnp.sort(borders).astype(jnp.int32)
    starts = jnp.concatenate([jnp.zeros((1,), jnp.int32), borders])
    finishes = jnp.concatenate([borders, jnp.full((1,), NBLK, jnp.int32)])
    return jnp.stack([starts, finishes], axis=1)


def shard_levels(rng, shape, shards, least, high):
    gain = 1.0
    for axis_at, parts in shards:
        steps = jax.random.uniform(jax.random.fold_in(jax.random.fold_in(rng, 6), axis_at), (parts,), jnp.float32, least / len(shards), high / len(shards))
        gain = gain * jnp.repeat(jnp.exp(steps), shape[axis_at] // parts).reshape((-1,) + (1,) * (len(shape) - 1 - axis_at))
    return gain


def gaussian(rng, shape, deviation, bound, shards=(), held_as=jnp.bfloat16):
    values = jax.random.normal(rng, shape, jnp.float32) * deviation
    if len(shards) > 0:
        values = shard_levels(rng, shape, shards, -0.22, 0.18) * values
    return jnp.clip(values, min=-bound, max=bound).astype(held_as)


def setup_inputs(seed: int = 0) -> dict:
    seeds = jax.random.split(jax.random.key(seed), 8)
    queries = gaussian(seeds[0], (LEN, HD), 1.0, 6.0, ((0, 16), (1, 2)))
    keys = gaussian(seeds[1], (LEN, HD), 1.0, 6.0, ((0, 16), (1, 2)))
    values = gaussian(seeds[2], (LEN, HD), 1.0, 6.0, ((0, 16), (1, 2)))
    feature_weight = gaussian(seeds[3], (H, HS, HS), HS ** -0.5, 0.5, ((1, 2), (2, 16)))
    norm_gain = jnp.clip(1.0 + 0.18 * jax.random.normal(seeds[4], (H, HS), jnp.float32), 0.099609375, 1.8984375).astype(jnp.bfloat16)
    doc_bounds = draw_doc_bounds(jax.random.fold_in(seeds[7], 71), 0)
    out_grad = gaussian(seeds[6], (LEN, HD), 1.0, 6.0, ((0, 16), (1, 2)))
    return dict(queries=queries, keys=keys, values=values, feature_weight=feature_weight, norm_gain=norm_gain, doc_bounds=doc_bounds, out_grad=out_grad)


epsilon = 1.0

def rounded(array):
    return lax.optimization_barrier(array.astype(jnp.bfloat16)).astype(jnp.float32)

def one_head(starts_here, items):
    query_rows, key_rows, value_rows, grad_rows, weight_f, gain_f = items
    block_shape = (NBLK, BLK, HS)
    query_blocks = query_rows.reshape(block_shape).astype(jnp.float32)
    key_blocks = key_rows.reshape(block_shape).astype(jnp.float32)
    value_blocks = value_rows.reshape(block_shape).astype(jnp.float32)
    grad_y = grad_rows.reshape(block_shape).astype(jnp.float32)
    qfeat = rounded(jnp.einsum('btd,de->bte', query_blocks, weight_f))
    kfeat = rounded(jnp.einsum('btd,de->bte', key_blocks, weight_f))
    updates = jnp.einsum('bte,btf->bef', kfeat, value_blocks)
    zero_state = jnp.zeros((HS, HS), jnp.float32)

    def forward_step(running, item):
        update, opened = item
        held = jnp.where(opened, zero_state, running)
        return (held + update, held)
    _, states = lax.scan(forward_step, zero_state, (updates, starts_here))
    state_half = rounded(states)
    causal = jnp.arange(BLK)[:, None] >= jnp.arange(BLK)[None, :]
    scores = jnp.einsum('bte,bse->bts', qfeat, kfeat)
    prob_half = rounded(jnp.where(causal, scores, 0.0))
    mixed_f = jnp.einsum('bte,bef->btf', qfeat, state_half) + jnp.einsum('bts,bsf->btf', prob_half, value_blocks)
    inverse = lax.rsqrt(lax.optimization_barrier(jnp.mean(mixed_f * mixed_f, axis=-1, keepdims=True)) + epsilon)
    mixed = (mixed_f * inverse * gain_f).astype(jnp.bfloat16)
    scaled = grad_y * gain_f
    grad_mix = inverse * (scaled - mixed_f * inverse * inverse * lax.optimization_barrier(jnp.mean(scaled * mixed_f, axis=-1, keepdims=True)))
    grad_half = rounded(grad_mix)
    gain_part = lax.optimization_barrier(jnp.sum(grad_y * mixed_f * inverse, axis=(0, 1)))
    state_grads = jnp.einsum('bte,btf->bef', qfeat, grad_half)

    def backward_step(running, item):
        grad_term, opened = item
        return (jnp.where(opened, zero_state, running + grad_term), running)
    _, suffix = lax.scan(backward_step, zero_state, (state_grads, starts_here), reverse=True)
    suffix_half = rounded(suffix)
    dot_grads = rounded(jnp.where(causal, jnp.einsum('btf,bsf->bts', grad_half, value_blocks), 0.0))
    qfeat_grad = rounded(jnp.einsum('btf,bef->bte', grad_half, state_half) + jnp.einsum('bts,bse->bte', dot_grads, kfeat))
    kfeat_grad = rounded(jnp.einsum('bsf,bef->bse', value_blocks, suffix_half) + jnp.einsum('bts,bte->bse', dot_grads, qfeat))
    value_grad = (jnp.einsum('bse,bef->bsf', kfeat, suffix_half) + jnp.einsum('bts,btf->bsf', prob_half, grad_half)).astype(jnp.bfloat16)
    query_grad = jnp.einsum('bte,de->btd', qfeat_grad, weight_f).astype(jnp.bfloat16)
    key_grad = jnp.einsum('bte,de->btd', kfeat_grad, weight_f).astype(jnp.bfloat16)
    weight_part = jnp.einsum('btd,bte->de', query_blocks, qfeat_grad) + jnp.einsum('btd,bte->de', key_blocks, kfeat_grad)
    flat_shape = (LEN, HS)
    return (mixed.reshape(flat_shape), query_grad.reshape(flat_shape), key_grad.reshape(flat_shape), value_grad.reshape(flat_shape), weight_part, gain_part)

def to_heads(rows):
    return rows.reshape(LEN, H, HS).transpose(1, 0, 2)

def from_heads(stacked):
    return stacked.transpose(1, 0, 2).reshape(LEN, H * HS)

def reference(queries, keys, values, feature_weight, norm_gain, doc_bounds, out_grad):
    block_ids = jnp.arange(NBLK, dtype=jnp.int32)
    starts_here = jnp.any(doc_bounds[:, 0].astype(jnp.int32)[None, :] == block_ids[:, None], axis=1)
    items = (to_heads(queries), to_heads(keys), to_heads(values), to_heads(out_grad), feature_weight.astype(jnp.float32), norm_gain.astype(jnp.float32))
    results = lax.map(partial(one_head, starts_here), items)
    mixed, query_grad, key_grad, value_grad, weight_parts, gain_parts = results
    factor = LEN ** (-0.5)
    return (from_heads(mixed), from_heads(query_grad), from_heads(key_grad), from_heads(value_grad), weight_parts * factor, gain_parts * factor)
```

```python
import functools

import jax
import jax.numpy as jnp
from jax import lax
from jax.experimental import pallas as pl
from jax.experimental.pallas import tpu as pltpu
from jax.sharding import PartitionSpec as P

HS = 128
BLK = 128


epsilon = 1.0


def carried_in(shard, axis, join, neutral, backward):
    count = lax.axis_size(axis)
    place = lax.axis_index(axis)
    ahead = count - 1 - place if backward else place
    gathered = jax.tree.map(
        lambda a, kind: lax.all_gather(a.astype(kind), axis), shard, (jnp.bfloat16, jnp.bfloat16)
    )
    state = jax.tree.map(lambda a, e: jnp.zeros_like(a) + jnp.asarray(e, a.dtype), shard, neutral)

    def one(hop, state):
        source = count - 1 - hop if backward else hop
        return join(
            state,
            jax.tree.map(
                lambda a, own: lax.dynamic_index_in_dim(a, source, 0, False).astype(own.dtype),
                gathered,
                shard,
            ),
        )

    return lax.fori_loop(0, ahead, one, state)


def chain_states(earlier, later):
    early_state, early_flag = earlier
    late_state, late_flag = later
    return (
        jnp.where(late_flag > 0.0, late_state, early_state + late_state),
        jnp.maximum(early_flag, late_flag),
    )


def project(rows, weight):
    return jnp.einsum("bthd,hde->bthe", rows, weight, preferred_element_type=jnp.float32).astype(
        jnp.bfloat16
    )


def plain(queries, keys, values, feature_weight, norm_gain, doc_bounds, out_grad):
    rows_full = lax.all_gather(feature_weight, "seq", axis=2, tiled=True)
    weight_local = lax.all_to_all(rows_full, "fsdp", split_axis=0, concat_axis=1, tiled=True)
    head_count = weight_local.shape[0]
    tokens_here = queries.shape[0]
    block_count = tokens_here // BLK
    block_shape = (block_count, BLK, head_count, HS)
    query_blocks = queries.reshape(block_shape)
    key_blocks = keys.reshape(block_shape)
    value_blocks = values.reshape(block_shape)
    qfeat = project(query_blocks, weight_local)
    kfeat = project(key_blocks, weight_local)
    first_block = lax.axis_index("seq") * block_count
    block_ids = first_block + jnp.arange(block_count, dtype=jnp.int32)
    starts = doc_bounds[:, 0]
    starts_here = jnp.any(starts[None, :] == block_ids[:, None], axis=1)
    opened = jnp.cumsum(starts_here.astype(jnp.int32))
    reach_left = opened == 0
    reach_right = opened[-1] - opened == 0
    has_start = jnp.any(starts_here).astype(jnp.float32)
    updates = jnp.einsum("bthe,bthf->bhef", kfeat, value_blocks, preferred_element_type=jnp.float32)
    zero_state = jnp.zeros(updates.shape[1:], jnp.float32)
    zero_flag = jnp.zeros((), jnp.float32)
    running = zero_state
    prefix_list = []
    for position in range(block_count):
        held = jnp.where(starts_here[position], zero_state, running)
        prefix_list.append(held)
        running = held + updates[position]
    entering, _ = carried_in(
        (running, has_start), "seq", chain_states, (zero_state, zero_flag), False
    )
    states = jnp.stack(prefix_list) + jnp.where(
        reach_left[:, None, None, None], entering[None], 0.0
    )
    state_half = states.astype(jnp.bfloat16)
    causal = jnp.arange(BLK)[:, None] >= jnp.arange(BLK)[None, :]
    scores = jnp.einsum("bthe,bshe->bhts", qfeat, kfeat, preferred_element_type=jnp.float32)
    prob_half = jnp.where(causal, scores, 0.0).astype(jnp.bfloat16)
    mixed_f = jnp.einsum("bthe,bhef->bthf", qfeat, state_half, preferred_element_type=jnp.float32)
    mixed_f = mixed_f + jnp.einsum(
        "bhts,bshf->bthf", prob_half, value_blocks, preferred_element_type=jnp.float32
    )
    gains = norm_gain.astype(jnp.float32)
    inverse = lax.rsqrt(jnp.mean(mixed_f * mixed_f, axis=-1, keepdims=True) + epsilon)
    mixed = (mixed_f * inverse * gains).astype(jnp.bfloat16)
    grad_y = out_grad.reshape(block_shape).astype(jnp.float32)
    scaled = grad_y * gains
    grad_mix = inverse * (
        scaled - mixed_f * inverse * inverse * jnp.mean(scaled * mixed_f, axis=-1, keepdims=True)
    )
    grad_half = grad_mix.astype(jnp.bfloat16)
    gain_part = jnp.sum(grad_y * mixed_f * inverse, axis=(0, 1))
    state_grads = jnp.einsum(
        "bthe,bthf->bhef", qfeat, grad_half, preferred_element_type=jnp.float32
    )
    running = zero_state
    suffix_list = [zero_state] * block_count
    for position in reversed(range(block_count)):
        suffix_list[position] = running
        running = jnp.where(starts_here[position], zero_state, running + state_grads[position])
    leaving, _ = carried_in(
        (running, has_start), "seq", chain_states, (zero_state, zero_flag), True
    )
    suffix = jnp.stack(suffix_list) + jnp.where(
        reach_right[:, None, None, None], leaving[None], 0.0
    )
    suffix_half = suffix.astype(jnp.bfloat16)
    dot_grads = jnp.einsum(
        "bthf,bshf->bhts", grad_half, value_blocks, preferred_element_type=jnp.float32
    )
    dot_half = jnp.where(causal, dot_grads, 0.0).astype(jnp.bfloat16)
    qfeat_grad = jnp.einsum(
        "bthf,bhef->bthe", grad_half, state_half, preferred_element_type=jnp.float32
    )
    qfeat_grad = (
        qfeat_grad
        + jnp.einsum("bhts,bshe->bthe", dot_half, kfeat, preferred_element_type=jnp.float32)
    ).astype(jnp.bfloat16)
    kfeat_grad = jnp.einsum(
        "bshf,bhef->bshe", value_blocks, suffix_half, preferred_element_type=jnp.float32
    )
    kfeat_grad = (
        kfeat_grad
        + jnp.einsum("bhts,bthe->bshe", dot_half, qfeat, preferred_element_type=jnp.float32)
    ).astype(jnp.bfloat16)
    value_grad = jnp.einsum(
        "bshe,bhef->bshf", kfeat, suffix_half, preferred_element_type=jnp.float32
    )
    value_grad = (
        value_grad
        + jnp.einsum("bhts,bthf->bshf", prob_half, grad_half, preferred_element_type=jnp.float32)
    ).astype(jnp.bfloat16)
    query_grad = jnp.einsum(
        "bthe,hde->bthd", qfeat_grad, weight_local, preferred_element_type=jnp.float32
    ).astype(jnp.bfloat16)
    key_grad = jnp.einsum(
        "bthe,hde->bthd", kfeat_grad, weight_local, preferred_element_type=jnp.float32
    ).astype(jnp.bfloat16)
    weight_part = jnp.einsum(
        "bthd,bthe->hde", query_blocks, qfeat_grad, preferred_element_type=jnp.float32
    )
    weight_part = weight_part + jnp.einsum(
        "bthd,bthe->hde", key_blocks, kfeat_grad, preferred_element_type=jnp.float32
    )
    weight_sum, gain_sum = lax.psum((weight_part, gain_part), "seq")
    column_width = weight_sum.shape[2] // lax.axis_size("seq")
    weight_columns = lax.dynamic_slice_in_dim(
        weight_sum, lax.axis_index("seq") * column_width, column_width, 2
    )
    owned_grad = lax.all_to_all(weight_columns, "fsdp", split_axis=1, concat_axis=0, tiled=True)
    factor = (lax.axis_size("seq") * tokens_here) ** (-0.5)
    flat_shape = (tokens_here, head_count * HS)
    return (
        mixed.reshape(flat_shape),
        query_grad.reshape(flat_shape),
        key_grad.reshape(flat_shape),
        value_grad.reshape(flat_shape),
        owned_grad * factor,
        gain_sum * factor,
    )

MESH = pl.DeviceIdType.MESH


def nn(a, b):
    return lax.dot_general(a, b, (((1,), (0,)), ((), ())), preferred_element_type=jnp.float32)


def nt(a, b):
    return lax.dot_general(a, b, (((1,), (1,)), ((), ())), preferred_element_type=jnp.float32)


def tn(a, b):
    return lax.dot_general(a, b, (((0,), (0,)), ((), ())), preferred_element_type=jnp.float32)


def layer_kernel(
    n, heads, blocks, docs, factor,
    bounds, q, k, v, og, gain, wx,
    mixed, qgrad, kgrad, vgrad, wout, gout,
    gain_f, wslab, wpart, gw, wt, mloc, mtot, rx, tx, back,
    qf, kf, prob, oin, sh, dh, eloc, etot, rx2, tx2, back2,
    dotq, dqf, dkf, dkp, vgp, wgt, wgs, rwg, gl, gp, fin, rfin,
    w_s, w_r, g_s, g_r, m_s, m_r, b_s, b_r, e_s, e_r, c_s, c_r, p_s, p_r, t_s, t_r, f_s, f_r,
):
    me = lax.axis_index("seq")
    mine = lax.axis_index("fsdp")
    partner = 1 - mine
    per_head = n // heads
    slab = HS // per_head
    width = HS // n
    groups = t_s.shape[0]
    group_rows = heads * width // groups

    barrier = pltpu.get_barrier_semaphore()

    def greet(step, carry):
        pl.semaphore_signal(
            barrier, inc=1, device_id={"seq": lax.rem(me + step, n)}, device_id_type=MESH
        )
        return carry

    lax.fori_loop(1, n, greet, 0)
    pl.semaphore_signal(barrier, inc=1, device_id={"fsdp": partner}, device_id_type=MESH)

    def push(src, dst, send, recv, p):
        return pltpu.make_async_remote_copy(
            src_ref=src, dst_ref=dst, send_sem=send, recv_sem=recv,
            device_id={"seq": p}, device_id_type=MESH,
        )

    def opens_in(first, count):
        found = jnp.float32(0.0)
        for i in range(docs):
            s = bounds[i, 0]
            found = jnp.where(jnp.logical_and(s >= first, s < first + count), 1.0, found)
        return found

    def columns(h):
        return pl.ds(pl.multiple_of(h * HS, HS), HS)

    def rows(b):
        return pl.ds(b * BLK, BLK)

    cont = [1.0 - opens_in(me * blocks + b, 1) for b in range(blocks)]
    reach_left = []
    value = jnp.float32(1.0)
    for b in range(blocks):
        value = value * cont[b]
        reach_left.append(value)
    reach_right = [None] * blocks
    value = jnp.float32(1.0)
    for b in reversed(range(blocks)):
        reach_right[b] = value
        value = value * cont[b]

    gain_f[...] = gain[...].astype(jnp.float32)

    def outer_products(h, carry):
        run = jnp.zeros((HS, HS), jnp.float32)
        for b in range(blocks):
            held = run * cont[b]
            mloc[b, h] = held
            run = held + tn(k[rows(b), columns(h)], v[rows(b), columns(h)])
        mtot[pl.ds(h * per_head, per_head)] = run.reshape(per_head, slab, HS).astype(jnp.bfloat16)
        return carry

    lax.fori_loop(0, heads, outer_products, 0)
    pl.semaphore_wait(barrier, n)

    weight_swap = pltpu.make_async_remote_copy(
        src_ref=wx.at[partner], dst_ref=wpart, send_sem=w_s, recv_sem=w_r,
        device_id={"fsdp": partner}, device_id_type=MESH,
    )
    weight_swap.start()

    def send_totals(step, carry):
        p = lax.rem(me + step, n)
        push(mtot.at[p], rx.at[me], m_s.at[p], m_r.at[me], p).start()
        return carry

    lax.fori_loop(1, n, send_totals, 0)
    weight_swap.wait()
    lane = lax.broadcasted_iota(jnp.int32, wslab.shape, 1)
    own_lane = (lane // (HS // 2)) == mine
    wslab[...] = jnp.where(
        own_lane, wx[mine].astype(jnp.float32), wpart[...].astype(jnp.float32)
    ).astype(jnp.bfloat16)

    def send_weights(step, carry):
        p = lax.rem(me + step, n)
        push(wslab, gw.at[me], g_s.at[p], g_r.at[me], p).start()
        return carry

    lax.fori_loop(1, n, send_weights, 0)
    gw[me] = wslab[...]

    def scan(total, arrived, parts, entered, in_s, in_r, out_s, out_r, backward):
        arrived[me] = total[me]

        def one(step, state):
            p = n - 1 - step if backward else step

            @pl.when(p != me)
            def _():
                push(total.at[p], arrived.at[p], in_s.at[p], in_r.at[p], p).wait_recv()

            parts[p] = state.astype(jnp.bfloat16)

            @pl.when(p != me)
            def _():
                push(parts.at[p], entered.at[me], out_s.at[p], out_r.at[me], p).start()

            keep = 1.0 - opens_in(p * blocks, blocks)
            return state * keep + arrived[p].astype(jnp.float32)

        lax.fori_loop(0, n, one, jnp.zeros((slab, HS), jnp.float32))
        entered[me] = parts[me]

    def entering(h, parts, entered, out_s, out_r):
        for j in range(per_head):
            p = h * per_head + j

            @pl.when(p != me)
            def _():
                push(parts.at[p], entered.at[p], out_s.at[p], out_r.at[p], p).wait_recv()

        return entered[pl.ds(h * per_head, per_head)].astype(jnp.float32).reshape(HS, HS)

    scan(mtot, rx, tx, back, m_s, m_r, b_s, b_r, False)

    def await_weights(step, carry):
        p = lax.rem(me + n - step, n)
        push(wslab, gw.at[p], g_s.at[p], g_r.at[p], p).wait_recv()
        return carry

    lax.fori_loop(1, n, await_weights, 0)
    causal = lax.broadcasted_iota(jnp.int32, (BLK, BLK), 0) >= lax.broadcasted_iota(
        jnp.int32, (BLK, BLK), 1
    )

    def project_pair(pair, carry):
        both = gw[:, pl.ds(pl.multiple_of(pair * 2 * width, 2 * width), 2 * width), :]
        both = both.astype(jnp.float32)
        for j in range(2):
            h = 2 * pair + j
            weight = both[:, j * width : (j + 1) * width, :].reshape(HS, HS).astype(jnp.bfloat16)
            wt[h] = weight
            qh = nt(q[:, columns(h)], weight).astype(jnp.bfloat16)
            kh = nt(k[:, columns(h)], weight).astype(jnp.bfloat16)
            qf[h] = qh
            kf[h] = kh
            for b in range(blocks):
                at = slice(b * BLK, (b + 1) * BLK)
                scores = jnp.where(causal, nt(qh[at], kh[at]), 0.0).astype(jnp.bfloat16)
                prob[h, rows(b), :] = scores
                oin[h, rows(b), :] = nn(scores, v[rows(b), columns(h)])
        return carry

    lax.fori_loop(0, heads // 2, project_pair, 0)

    def forward(h, carry):
        enter = entering(h, tx, back, b_s, b_r)
        weight = wt[h]
        g = gain_f[pl.ds(h, 1), :]
        terms = []
        gain_sum = jnp.zeros((1, HS), jnp.float32)
        for b in range(blocks):
            memory = (mloc[b, h] + reach_left[b] * enter).astype(jnp.bfloat16)
            state = nn(weight, memory).astype(jnp.bfloat16)
            sh[b, h] = state
            qb = qf[h, rows(b), :]
            o = oin[h, rows(b), :] + nn(qb, state)
            r = lax.rsqrt(jnp.mean(o * o, axis=-1, keepdims=True) + epsilon)
            normed = o * r
            mixed[rows(b), columns(h)] = (normed * g).astype(jnp.bfloat16)
            gy = og[rows(b), columns(h)].astype(jnp.float32)
            scaled = gy * g
            inner = jnp.mean(scaled * o, axis=-1, keepdims=True)
            d = (r * (scaled - normed * (r * inner))).astype(jnp.bfloat16)
            dh[h, rows(b), :] = d
            gain_sum = gain_sum + jnp.sum(gy * normed, axis=0, keepdims=True)
            terms.append(tn(qb, d))
        gl[pl.ds(h, 1), :] = gain_sum
        run = jnp.zeros((HS, HS), jnp.float32)
        for b in reversed(range(blocks)):
            eloc[b, h] = run
            run = (run + terms[b]) * cont[b]
        etot[pl.ds(h * per_head, per_head)] = run.reshape(per_head, slab, HS).astype(jnp.bfloat16)
        for j in range(per_head):
            p = h * per_head + j

            @pl.when(p != me)
            def _():
                push(etot.at[p], rx2.at[me], e_s.at[p], e_r.at[me], p).start()

        return carry

    lax.fori_loop(0, heads, forward, 0)

    def send_gain(step, carry):
        p = lax.rem(me + step, n)
        push(gl, gp.at[me], p_s.at[p], p_r.at[me], p).start()
        return carry

    lax.fori_loop(1, n, send_gain, 0)
    gp[me] = gl[...]

    def query_side(h, carry):
        for b in range(blocks):
            d = dh[h, rows(b), :]
            scores = jnp.where(causal, nt(d, v[rows(b), columns(h)]), 0.0).astype(jnp.bfloat16)
            dotq[h, rows(b), :] = scores
            dqf[rows(b), :] = (nt(d, sh[b, h]) + nn(scores, kf[h, rows(b), :])).astype(jnp.bfloat16)
        grads = dqf[...]
        qgrad[:, columns(h)] = nn(grads, wt[h]).astype(jnp.bfloat16)
        wgt[h] = tn(grads, q[:, columns(h)])
        return carry

    lax.fori_loop(0, heads, query_side, 0)
    scan(etot, rx2, tx2, back2, e_s, e_r, c_s, c_r, True)

    def local_key_side(h, carry):
        for b in range(blocks):
            dkp[h, rows(b), :] = tn(dotq[h, rows(b), :], qf[h, rows(b), :])
            vgp[h, rows(b), :] = tn(prob[h, rows(b), :], dh[h, rows(b), :])
        return carry

    lax.fori_loop(0, heads, local_key_side, 0)

    def key_side(h):
        enter = entering(h, tx2, back2, c_s, c_r)
        for b in range(blocks):
            memory = (eloc[b, h] + reach_right[b] * enter).astype(jnp.bfloat16)
            vb = v[rows(b), columns(h)]
            dkf[rows(b), :] = (nt(vb, memory) + dkp[h, rows(b), :]).astype(jnp.bfloat16)
            vgrad[rows(b), columns(h)] = (
                nn(kf[h, rows(b), :], memory) + vgp[h, rows(b), :]
            ).astype(jnp.bfloat16)
        grads = dkf[...]
        kgrad[:, columns(h)] = nn(grads, wt[h]).astype(jnp.bfloat16)
        return (wgt[h] + tn(grads, k[:, columns(h)])).reshape(n, width, HS)

    pairs = heads // 2 // groups

    def key_group(group, carry):
        def key_pair(i, inner):
            pair = group * pairs + i
            both = jnp.concatenate([key_side(2 * pair), key_side(2 * pair + 1)], axis=1)
            wgs[group, :, pl.ds(pl.multiple_of(i * 2 * width, 2 * width), 2 * width), :] = (
                both.astype(jnp.bfloat16)
            )
            return inner

        lax.fori_loop(0, pairs, key_pair, 0)

        def send_terms(step, inner):
            p = lax.rem(me + step, n)
            push(
                wgs.at[group, p], rwg.at[group, me], t_s.at[group, p], t_r.at[group, me], p
            ).start()
            return inner

        lax.fori_loop(1, n, send_terms, 0)
        rwg[group, me] = wgs[group, me]
        return carry

    lax.fori_loop(0, groups, key_group, 0)

    def add_gain(step, carry):
        p = lax.rem(me + n - step, n)
        push(gl, gp.at[p], p_s.at[p], p_r.at[p], p).wait_recv()
        return carry

    lax.fori_loop(1, n, add_gain, 0)
    gout[...] = jnp.sum(gp[...], axis=0) * factor

    for group in range(groups):

        def arrive(step, total):
            p = lax.rem(me + n - step, n)
            push(
                wgs.at[group, p], rwg.at[group, p], t_s.at[group, p], t_r.at[group, p], p
            ).wait_recv()
            return total + rwg[group, p].astype(jnp.float32)

        total = lax.fori_loop(1, n, arrive, rwg[group, me].astype(jnp.float32))
        fin[pl.ds(group * group_rows, group_rows), :] = total * factor

    owned_swap = pltpu.make_async_remote_copy(
        src_ref=fin, dst_ref=rfin, send_sem=f_s, recv_sem=f_r,
        device_id={"fsdp": partner}, device_id_type=MESH,
    )
    owned_swap.start()
    wout[mine] = fin[...]

    def sent(step, carry):
        p = lax.rem(me + step, n)
        push(mtot.at[p], rx.at[me], m_s.at[p], m_r.at[me], p).wait_send()
        push(wslab, gw.at[me], g_s.at[p], g_r.at[me], p).wait_send()
        push(tx.at[p], back.at[me], b_s.at[p], b_r.at[me], p).wait_send()
        push(etot.at[p], rx2.at[me], e_s.at[p], e_r.at[me], p).wait_send()
        push(tx2.at[p], back2.at[me], c_s.at[p], c_r.at[me], p).wait_send()
        push(gl, gp.at[me], p_s.at[p], p_r.at[me], p).wait_send()
        for group in range(groups):
            push(
                wgs.at[group, p], rwg.at[group, me], t_s.at[group, p], t_r.at[group, me], p
            ).wait_send()
        return carry

    lax.fori_loop(1, n, sent, 0)
    owned_swap.wait()
    wout[partner] = rfin[...]


def fused(n, queries, keys, values, feature_weight, norm_gain, doc_bounds, out_grad):
    tokens, features = queries.shape
    heads = features // HS
    blocks = tokens // BLK
    width = HS // n
    deep = feature_weight.shape[1]
    rows_each = heads * HS // n
    slab_rows = heads * width
    groups = 2
    turned = jnp.swapaxes(feature_weight, 1, 2).reshape(2, slab_rows, deep)
    wx = jnp.concatenate([turned, turned], axis=2)
    factor = float((n * tokens) ** -0.5)
    bf, f32 = jnp.bfloat16, jnp.float32
    vm = pltpu.VMEM
    per = (heads, tokens, HS)
    slabs = (n, rows_each, HS)
    scratch = [
        vm((heads, HS), f32), vm((slab_rows, HS), bf), vm((slab_rows, HS), bf),
        vm((n, slab_rows, HS), bf), vm((heads, HS, HS), bf),
        vm((blocks, heads, HS, HS), f32),
        vm(slabs, bf), vm(slabs, bf), vm(slabs, bf), vm(slabs, bf),
        vm(per, bf), vm(per, bf), vm(per, bf), vm(per, f32),
        vm((blocks, heads, HS, HS), bf), vm(per, bf), vm((blocks, heads, HS, HS), f32),
        vm(slabs, bf), vm(slabs, bf), vm(slabs, bf), vm(slabs, bf),
        vm(per, bf), vm((tokens, HS), bf), vm((tokens, HS), bf), vm(per, f32), vm(per, f32),
        vm((heads, HS, HS), f32),
        vm((groups, n, slab_rows // groups, HS), bf), vm((groups, n, slab_rows // groups, HS), bf),
        vm((heads, HS), f32), vm((n, heads, HS), f32),
        vm((slab_rows, HS), f32), vm((slab_rows, HS), f32),
    ]
    dma = pltpu.SemaphoreType.DMA
    sems = [dma, dma] + [dma((n,))] * 12 + [dma((groups, n))] * 2 + [dma, dma]
    flat = jax.ShapeDtypeStruct((tokens, features), bf)
    in_vmem = pl.BlockSpec(memory_space=vm)
    mixed, qgrad, kgrad, vgrad, wout, gout = pl.pallas_call(
        functools.partial(layer_kernel, n, heads, blocks, doc_bounds.shape[0], factor),
        out_shape=(
            flat, flat, flat, flat,
            jax.ShapeDtypeStruct((2, slab_rows, HS), f32),
            jax.ShapeDtypeStruct((heads, HS), f32),
        ),
        in_specs=[pl.BlockSpec(memory_space=pltpu.SMEM)] + [in_vmem] * 6,
        out_specs=(in_vmem,) * 6,
        scratch_shapes=scratch + sems,
        compiler_params=pltpu.CompilerParams(
            collective_id=0, has_side_effects=True, vmem_limit_bytes=52 * 2**20
        ),
        cost_estimate=pl.CostEstimate(
            flops=36 * tokens * features * HS, bytes_accessed=16 * tokens * features,
            transcendentals=0,
        ),
        name="layer",
    )(doc_bounds, queries, keys, values, out_grad, norm_gain, wx)
    owned = wout.reshape(2 * heads, width, HS)
    owned = lax.dynamic_slice_in_dim(owned, lax.axis_index("fsdp") * deep, deep, 2)
    return mixed, qgrad, kgrad, vgrad, jnp.swapaxes(owned, 1, 2), gout


def local(*args):
    n = lax.axis_size("seq")
    heads = args[0].shape[1] // HS
    width = HS // n
    if lax.axis_size("fsdp") == 2 and width == 8 and n % heads == 0 and heads % 4 == 0:
        return fused(n, *args)
    return plain(*args)


def solution(mesh):
    placed = (
        P("seq", "fsdp"),
        P("seq", "fsdp"),
        P("seq", "fsdp"),
        P(None, "fsdp", "seq"),
        P("fsdp", None),
        P(),
        P("seq", "fsdp"),
    )
    return jax.shard_map(
        local,
        mesh=mesh,
        in_specs=placed,
        out_specs=(
            P("seq", "fsdp"),
            P("seq", "fsdp"),
            P("seq", "fsdp"),
            P("seq", "fsdp"),
            P(None, "fsdp", "seq"),
            P("fsdp", None),
        ),
        check_vma=False,
    )
```

```python
import functools

import jax
import jax.numpy as jnp
from jax import lax
from jax.experimental import pallas as pl
from jax.experimental.pallas import tpu as pltpu
from jax.sharding import PartitionSpec as P

HS = 128
BLK = 128


epsilon = 1.0


def carried_in(shard, axis, join, neutral, backward):
    count = lax.axis_size(axis)
    place = lax.axis_index(axis)
    ahead = count - 1 - place if backward else place
    gathered = jax.tree.map(
        lambda a, kind: lax.all_gather(a.astype(kind), axis), shard, (jnp.bfloat16, jnp.bfloat16)
    )
    state = jax.tree.map(lambda a, e: jnp.zeros_like(a) + jnp.asarray(e, a.dtype), shard, neutral)

    def one(hop, state):
        source = count - 1 - hop if backward else hop
        return join(
            state,
            jax.tree.map(
                lambda a, own: lax.dynamic_index_in_dim(a, source, 0, False).astype(own.dtype),
                gathered,
                shard,
            ),
        )

    return lax.fori_loop(0, ahead, one, state)


def chain_states(earlier, later):
    early_state, early_flag = earlier
    late_state, late_flag = later
    return (
        jnp.where(late_flag > 0.0, late_state, early_state + late_state),
        jnp.maximum(early_flag, late_flag),
    )


def project(rows, weight):
    return jnp.einsum("bthd,hde->bthe", rows, weight, preferred_element_type=jnp.float32).astype(
        jnp.bfloat16
    )


def plain(queries, keys, values, feature_weight, norm_gain, doc_bounds, out_grad):
    rows_full = lax.all_gather(feature_weight, "seq", axis=2, tiled=True)
    weight_local = lax.all_to_all(rows_full, "fsdp", split_axis=0, concat_axis=1, tiled=True)
    head_count = weight_local.shape[0]
    tokens_here = queries.shape[0]
    block_count = tokens_here // BLK
    block_shape = (block_count, BLK, head_count, HS)
    query_blocks = queries.reshape(block_shape)
    key_blocks = keys.reshape(block_shape)
    value_blocks = values.reshape(block_shape)
    qfeat = project(query_blocks, weight_local)
    kfeat = project(key_blocks, weight_local)
    first_block = lax.axis_index("seq") * block_count
    block_ids = first_block + jnp.arange(block_count, dtype=jnp.int32)
    starts = doc_bounds[:, 0]
    starts_here = jnp.any(starts[None, :] == block_ids[:, None], axis=1)
    opened = jnp.cumsum(starts_here.astype(jnp.int32))
    reach_left = opened == 0
    reach_right = opened[-1] - opened == 0
    has_start = jnp.any(starts_here).astype(jnp.float32)
    updates = jnp.einsum("bthe,bthf->bhef", kfeat, value_blocks, preferred_element_type=jnp.float32)
    zero_state = jnp.zeros(updates.shape[1:], jnp.float32)
    zero_flag = jnp.zeros((), jnp.float32)
    running = zero_state
    prefix_list = []
    for position in range(block_count):
        held = jnp.where(starts_here[position], zero_state, running)
        prefix_list.append(held)
        running = held + updates[position]
    entering, _ = carried_in(
        (running, has_start), "seq", chain_states, (zero_state, zero_flag), False
    )
    states = jnp.stack(prefix_list) + jnp.where(
        reach_left[:, None, None, None], entering[None], 0.0
    )
    state_half = states.astype(jnp.bfloat16)
    causal = jnp.arange(BLK)[:, None] >= jnp.arange(BLK)[None, :]
    scores = jnp.einsum("bthe,bshe->bhts", qfeat, kfeat, preferred_element_type=jnp.float32)
    prob_half = jnp.where(causal, scores, 0.0).astype(jnp.bfloat16)
    mixed_f = jnp.einsum("bthe,bhef->bthf", qfeat, state_half, preferred_element_type=jnp.float32)
    mixed_f = mixed_f + jnp.einsum(
        "bhts,bshf->bthf", prob_half, value_blocks, preferred_element_type=jnp.float32
    )
    gains = norm_gain.astype(jnp.float32)
    inverse = lax.rsqrt(jnp.mean(mixed_f * mixed_f, axis=-1, keepdims=True) + epsilon)
    mixed = (mixed_f * inverse * gains).astype(jnp.bfloat16)
    grad_y = out_grad.reshape(block_shape).astype(jnp.float32)
    scaled = grad_y * gains
    grad_mix = inverse * (
        scaled - mixed_f * inverse * inverse * jnp.mean(scaled * mixed_f, axis=-1, keepdims=True)
    )
    grad_half = grad_mix.astype(jnp.bfloat16)
    gain_part = jnp.sum(grad_y * mixed_f * inverse, axis=(0, 1))
    state_grads = jnp.einsum(
        "bthe,bthf->bhef", qfeat, grad_half, preferred_element_type=jnp.float32
    )
    running = zero_state
    suffix_list = [zero_state] * block_count
    for position in reversed(range(block_count)):
        suffix_list[position] = running
        running = jnp.where(starts_here[position], zero_state, running + state_grads[position])
    leaving, _ = carried_in(
        (running, has_start), "seq", chain_states, (zero_state, zero_flag), True
    )
    suffix = jnp.stack(suffix_list) + jnp.where(
        reach_right[:, None, None, None], leaving[None], 0.0
    )
    suffix_half = suffix.astype(jnp.bfloat16)
    dot_grads = jnp.einsum(
        "bthf,bshf->bhts", grad_half, value_blocks, preferred_element_type=jnp.float32
    )
    dot_half = jnp.where(causal, dot_grads, 0.0).astype(jnp.bfloat16)
    qfeat_grad = jnp.einsum(
        "bthf,bhef->bthe", grad_half, state_half, preferred_element_type=jnp.float32
    )
    qfeat_grad = (
        qfeat_grad
        + jnp.einsum("bhts,bshe->bthe", dot_half, kfeat, preferred_element_type=jnp.float32)
    ).astype(jnp.bfloat16)
    kfeat_grad = jnp.einsum(
        "bshf,bhef->bshe", value_blocks, suffix_half, preferred_element_type=jnp.float32
    )
    kfeat_grad = (
        kfeat_grad
        + jnp.einsum("bhts,bthe->bshe", dot_half, qfeat, preferred_element_type=jnp.float32)
    ).astype(jnp.bfloat16)
    value_grad = jnp.einsum(
        "bshe,bhef->bshf", kfeat, suffix_half, preferred_element_type=jnp.float32
    )
    value_grad = (
        value_grad
        + jnp.einsum("bhts,bthf->bshf", prob_half, grad_half, preferred_element_type=jnp.float32)
    ).astype(jnp.bfloat16)
    query_grad = jnp.einsum(
        "bthe,hde->bthd", qfeat_grad, weight_local, preferred_element_type=jnp.float32
    ).astype(jnp.bfloat16)
    key_grad = jnp.einsum(
        "bthe,hde->bthd", kfeat_grad, weight_local, preferred_element_type=jnp.float32
    ).astype(jnp.bfloat16)
    weight_part = jnp.einsum(
        "bthd,bthe->hde", query_blocks, qfeat_grad, preferred_element_type=jnp.float32
    )
    weight_part = weight_part + jnp.einsum(
        "bthd,bthe->hde", key_blocks, kfeat_grad, preferred_element_type=jnp.float32
    )
    weight_sum, gain_sum = lax.psum((weight_part, gain_part), "seq")
    column_width = weight_sum.shape[2] // lax.axis_size("seq")
    weight_columns = lax.dynamic_slice_in_dim(
        weight_sum, lax.axis_index("seq") * column_width, column_width, 2
    )
    owned_grad = lax.all_to_all(weight_columns, "fsdp", split_axis=1, concat_axis=0, tiled=True)
    factor = (lax.axis_size("seq") * tokens_here) ** (-0.5)
    flat_shape = (tokens_here, head_count * HS)
    return (
        mixed.reshape(flat_shape),
        query_grad.reshape(flat_shape),
        key_grad.reshape(flat_shape),
        value_grad.reshape(flat_shape),
        owned_grad * factor,
        gain_sum * factor,
    )

MESH = pl.DeviceIdType.MESH


def nn(a, b):
    return lax.dot_general(a, b, (((1,), (0,)), ((), ())), preferred_element_type=jnp.float32)


def nt(a, b):
    return lax.dot_general(a, b, (((1,), (1,)), ((), ())), preferred_element_type=jnp.float32)


def tn(a, b):
    return lax.dot_general(a, b, (((0,), (0,)), ((), ())), preferred_element_type=jnp.float32)


def layer_kernel(
    n, heads, blocks, docs, factor,
    bounds, q_in, k_in, v_in, og_in, gain, wx,
    mixed_out, qgrad_out, kgrad_out, vgrad_out, wout, gout,
    q, k, v, og, mixed, qgrad, kgrad, vgrad,
    gain_f, wslab, wpart, gw, wt, mloc, mtot, rx, tx, back,
    qf, kf, prob, sh, dh, eloc, etot, rx2, tx2, back2,
    dotq, dqf, dkp, vgp, wgt, wgs, rwg, gl, gp, fin, rfin,
    w_s, w_r, g_s, g_r, m_s, m_r, b_s, b_r, e_s, e_r, c_s, c_r, p_s, p_r, t_s, t_r, f_s, f_r, io,
):
    me = lax.axis_index("seq")
    mine = lax.axis_index("fsdp")
    partner = 1 - mine
    per_head = n // heads
    slab = HS // per_head
    width = HS // n
    groups = t_s.shape[0]
    group_rows = heads * width // groups

    barrier = pltpu.get_barrier_semaphore()

    def greet(step, carry):
        pl.semaphore_signal(
            barrier, inc=1, device_id={"seq": lax.rem(me + step, n)}, device_id_type=MESH
        )
        return carry

    lax.fori_loop(1, n, greet, 0)
    pl.semaphore_signal(barrier, inc=1, device_id={"fsdp": partner}, device_id_type=MESH)

    loads = [
        pltpu.make_async_copy(a, b, io.at[i])
        for i, (a, b) in enumerate([(k_in, k), (v_in, v), (q_in, q), (og_in, og)])
    ]
    for load in loads:
        load.start()
    stores = [
        pltpu.make_async_copy(a, b, io.at[4 + i])
        for i, (a, b) in enumerate(
            [(mixed, mixed_out), (qgrad, qgrad_out), (kgrad, kgrad_out), (vgrad, vgrad_out)]
        )
    ]

    def push(src, dst, send, recv, p):
        return pltpu.make_async_remote_copy(
            src_ref=src, dst_ref=dst, send_sem=send, recv_sem=recv,
            device_id={"seq": p}, device_id_type=MESH,
        )

    def opens_in(first, count):
        found = jnp.float32(0.0)
        for i in range(docs):
            s = bounds[i, 0]
            found = jnp.where(jnp.logical_and(s >= first, s < first + count), 1.0, found)
        return found

    def columns(h):
        return pl.ds(pl.multiple_of(h * HS, HS), HS)

    def rows(b):
        return pl.ds(b * BLK, BLK)

    cont = [1.0 - opens_in(me * blocks + b, 1) for b in range(blocks)]
    reach_left = []
    value = jnp.float32(1.0)
    for b in range(blocks):
        value = value * cont[b]
        reach_left.append(value)
    reach_right = [None] * blocks
    value = jnp.float32(1.0)
    for b in reversed(range(blocks)):
        reach_right[b] = value
        value = value * cont[b]

    gain_f[...] = gain[...].astype(jnp.float32)

    def outer_products(pair, carry):
        heads_here = (2 * pair, 2 * pair + 1)
        terms = [
            [tn(k[rows(b), columns(h)], v[rows(b), columns(h)]) for b in range(blocks)]
            for h in heads_here
        ]
        for h, term in zip(heads_here, terms):
            run = jnp.zeros((HS, HS), jnp.float32)
            for b in range(blocks):
                held = run * cont[b]
                mloc[b, h] = held
                run = held + term[b]
            mtot[pl.ds(h * per_head, per_head)] = run.reshape(per_head, slab, HS).astype(
                jnp.bfloat16
            )
        return carry

    loads[0].wait()
    loads[1].wait()
    lax.fori_loop(0, heads // 2, outer_products, 0)
    pl.semaphore_wait(barrier, n)

    weight_swap = pltpu.make_async_remote_copy(
        src_ref=wx.at[partner], dst_ref=wpart, send_sem=w_s, recv_sem=w_r,
        device_id={"fsdp": partner}, device_id_type=MESH,
    )
    weight_swap.start()

    def send_totals(step, carry):
        p = lax.rem(me + step, n)
        push(mtot.at[p], rx.at[me], m_s.at[p], m_r.at[me], p).start()
        return carry

    lax.fori_loop(1, n, send_totals, 0)
    weight_swap.wait()
    lane = lax.broadcasted_iota(jnp.int32, wslab.shape, 1)
    own_lane = (lane // (HS // 2)) == mine
    wslab[...] = jnp.where(
        own_lane, wx[mine].astype(jnp.float32), wpart[...].astype(jnp.float32)
    ).astype(jnp.bfloat16)

    def send_weights(step, carry):
        p = lax.rem(me + step, n)
        push(wslab, gw.at[me], g_s.at[p], g_r.at[me], p).start()
        return carry

    lax.fori_loop(1, n, send_weights, 0)
    gw[me] = wslab[...]

    def scan(total, arrived, parts, entered, in_s, in_r, out_s, out_r, backward):
        arrived[me] = total[me]

        def one(step, state):
            p = n - 1 - step if backward else step

            @pl.when(p != me)
            def _():
                push(total.at[p], arrived.at[p], in_s.at[p], in_r.at[p], p).wait_recv()

            parts[p] = state.astype(jnp.bfloat16)

            @pl.when(p != me)
            def _():
                push(parts.at[p], entered.at[me], out_s.at[p], out_r.at[me], p).start()

            keep = 1.0 - opens_in(p * blocks, blocks)
            return state * keep + arrived[p].astype(jnp.float32)

        lax.fori_loop(0, n, one, jnp.zeros((slab, HS), jnp.float32))
        entered[me] = parts[me]

    def entering(pair, parts, entered, out_s, out_r):
        for j in range(2 * per_head):
            p = pair * 2 * per_head + j

            @pl.when(p != me)
            def _():
                push(parts.at[p], entered.at[p], out_s.at[p], out_r.at[p], p).wait_recv()

        both = entered[pl.ds(pair * 2 * per_head, 2 * per_head)].astype(jnp.float32)
        return [both[:per_head].reshape(HS, HS), both[per_head:].reshape(HS, HS)]

    scan(mtot, rx, tx, back, m_s, m_r, b_s, b_r, False)

    def await_weights(step, carry):
        p = lax.rem(me + n - step, n)
        push(wslab, gw.at[p], g_s.at[p], g_r.at[p], p).wait_recv()
        return carry

    lax.fori_loop(1, n, await_weights, 0)
    causal = lax.broadcasted_iota(jnp.int32, (BLK, BLK), 0) >= lax.broadcasted_iota(
        jnp.int32, (BLK, BLK), 1
    )

    def project_pair(pair, carry):
        both = gw[:, pl.ds(pl.multiple_of(pair * 2 * width, 2 * width), 2 * width), :]
        both = both.astype(jnp.float32)
        features = []
        for j in range(2):
            h = 2 * pair + j
            weight = both[:, j * width : (j + 1) * width, :].reshape(HS, HS).astype(jnp.bfloat16)
            wt[h] = weight
            qh = nt(q[:, columns(h)], weight).astype(jnp.bfloat16)
            kh = nt(k[:, columns(h)], weight).astype(jnp.bfloat16)
            qf[h] = qh
            kf[h] = kh
            features.append((h, qh, kh))
        for h, qh, kh in features:
            for b in range(blocks):
                at = slice(b * BLK, (b + 1) * BLK)
                prob[h, rows(b), :] = jnp.where(causal, nt(qh[at], kh[at]), 0.0).astype(
                    jnp.bfloat16
                )
        return carry

    loads[2].wait()
    lax.fori_loop(0, heads // 2, project_pair, 0)
    loads[3].wait()

    def forward(pair, carry):
        enters = entering(pair, tx, back, b_s, b_r)
        heads_here = (2 * pair, 2 * pair + 1)
        states = []
        for h, enter in zip(heads_here, enters):
            memory = jnp.concatenate(
                [
                    (mloc[b, h] + reach_left[b] * enter).astype(jnp.bfloat16)
                    for b in range(blocks)
                ],
                axis=1,
            )
            states.append(nn(wt[h], memory).astype(jnp.bfloat16))
        outs = []
        for h, state in zip(heads_here, states):
            sh[h] = state
            for b in range(blocks):
                both = jnp.concatenate([qf[h, rows(b), :], prob[h, rows(b), :]], axis=1)
                held = jnp.concatenate(
                    [state[:, b * HS : (b + 1) * HS], v[rows(b), columns(h)]], axis=0
                )
                outs.append(nn(both, held))
        terms = []
        for i, h in enumerate(heads_here):
            g = gain_f[pl.ds(h, 1), :]
            gain_sum = jnp.zeros((1, HS), jnp.float32)
            for b in range(blocks):
                o = outs[i * blocks + b]
                r = lax.rsqrt(jnp.mean(o * o, axis=-1, keepdims=True) + epsilon)
                normed = o * r
                mixed[rows(b), columns(h)] = (normed * g).astype(jnp.bfloat16)
                gy = og[rows(b), columns(h)].astype(jnp.float32)
                scaled = gy * g
                inner = jnp.mean(scaled * o, axis=-1, keepdims=True)
                d = (r * (scaled - normed * (r * inner))).astype(jnp.bfloat16)
                dh[h, rows(b), :] = d
                gain_sum = gain_sum + jnp.sum(gy * normed, axis=0, keepdims=True)
                terms.append(tn(qf[h, rows(b), :], d))
            gl[pl.ds(h, 1), :] = gain_sum
        for i, h in enumerate(heads_here):
            run = jnp.zeros((HS, HS), jnp.float32)
            for b in reversed(range(blocks)):
                eloc[b, h] = run
                run = (run + terms[i * blocks + b]) * cont[b]
            etot[pl.ds(h * per_head, per_head)] = run.reshape(per_head, slab, HS).astype(
                jnp.bfloat16
            )
        for j in range(2 * per_head):
            p = pair * 2 * per_head + j

            @pl.when(p != me)
            def _():
                push(etot.at[p], rx2.at[me], e_s.at[p], e_r.at[me], p).start()

        return carry

    lax.fori_loop(0, heads // 2, forward, 0)
    stores[0].start()

    def send_gain(step, carry):
        p = lax.rem(me + step, n)
        push(gl, gp.at[me], p_s.at[p], p_r.at[me], p).start()
        return carry

    lax.fori_loop(1, n, send_gain, 0)
    gp[me] = gl[...]

    def query_side(pair, carry):
        heads_here = (2 * pair, 2 * pair + 1)
        for h in heads_here:
            scores = []
            for b in range(blocks):
                score = nt(dh[h, rows(b), :], v[rows(b), columns(h)])
                scores.append(jnp.where(causal, score, 0.0).astype(jnp.bfloat16))
            for b in range(blocks):
                dotq[h, rows(b), :] = scores[b]
                dqf[h, rows(b), :] = (
                    nt(dh[h, rows(b), :], sh[h, :, rows(b)]) + nn(scores[b], kf[h, rows(b), :])
                ).astype(jnp.bfloat16)
        return carry

    lax.fori_loop(0, heads // 2, query_side, 0)
    scan(etot, rx2, tx2, back2, e_s, e_r, c_s, c_r, True)

    def local_terms(pair, carry):
        for h in (2 * pair, 2 * pair + 1):
            grads = dqf[h]
            qgrad[:, columns(h)] = nn(grads, wt[h]).astype(jnp.bfloat16)
            wgt[h] = tn(grads, q[:, columns(h)])
            for b in range(blocks):
                dkp[h, rows(b), :] = tn(dotq[h, rows(b), :], qf[h, rows(b), :])
                vgp[h, rows(b), :] = tn(prob[h, rows(b), :], dh[h, rows(b), :])
        return carry

    lax.fori_loop(0, heads // 2, local_terms, 0)
    stores[1].start()

    def key_pair_grads(pair):
        enters = entering(pair, tx2, back2, c_s, c_r)
        heads_here = (2 * pair, 2 * pair + 1)
        grads = []
        for h, enter in zip(heads_here, enters):
            parts = []
            for b in range(blocks):
                memory = (eloc[b, h] + reach_right[b] * enter).astype(jnp.bfloat16)
                vb = v[rows(b), columns(h)]
                parts.append((nt(vb, memory) + dkp[h, rows(b), :]).astype(jnp.bfloat16))
                vgrad[rows(b), columns(h)] = (
                    nn(kf[h, rows(b), :], memory) + vgp[h, rows(b), :]
                ).astype(jnp.bfloat16)
            grads.append(jnp.concatenate(parts, axis=0))
        totals = []
        for h, grad in zip(heads_here, grads):
            kgrad[:, columns(h)] = nn(grad, wt[h]).astype(jnp.bfloat16)
            totals.append((wgt[h] + tn(grad, k[:, columns(h)])).reshape(n, width, HS))
        return jnp.concatenate(totals, axis=1)

    pairs = heads // 2 // groups

    def key_group(group, carry):
        def key_pair(i, inner):
            pair = group * pairs + i
            both = key_pair_grads(pair)
            wgs[group, :, pl.ds(pl.multiple_of(i * 2 * width, 2 * width), 2 * width), :] = (
                both.astype(jnp.bfloat16)
            )
            return inner

        lax.fori_loop(0, pairs, key_pair, 0)

        def send_terms(step, inner):
            p = lax.rem(me + step, n)
            push(
                wgs.at[group, p], rwg.at[group, me], t_s.at[group, p], t_r.at[group, me], p
            ).start()
            return inner

        lax.fori_loop(1, n, send_terms, 0)
        rwg[group, me] = wgs[group, me]
        return carry

    lax.fori_loop(0, groups, key_group, 0)
    stores[2].start()
    stores[3].start()

    def add_gain(step, carry):
        p = lax.rem(me + n - step, n)
        push(gl, gp.at[p], p_s.at[p], p_r.at[p], p).wait_recv()
        return carry

    lax.fori_loop(1, n, add_gain, 0)
    gout[...] = jnp.sum(gp[...], axis=0) * factor

    for group in range(groups):

        def arrive(step, total):
            p = lax.rem(me + n - step, n)
            push(
                wgs.at[group, p], rwg.at[group, p], t_s.at[group, p], t_r.at[group, p], p
            ).wait_recv()
            return total + rwg[group, p].astype(jnp.float32)

        total = lax.fori_loop(1, n, arrive, rwg[group, me].astype(jnp.float32))
        fin[pl.ds(group * group_rows, group_rows), :] = total * factor

    owned_swap = pltpu.make_async_remote_copy(
        src_ref=fin, dst_ref=rfin, send_sem=f_s, recv_sem=f_r,
        device_id={"fsdp": partner}, device_id_type=MESH,
    )
    owned_swap.start()
    wout[mine] = fin[...]

    def sent(step, carry):
        p = lax.rem(me + step, n)
        push(mtot.at[p], rx.at[me], m_s.at[p], m_r.at[me], p).wait_send()
        push(wslab, gw.at[me], g_s.at[p], g_r.at[me], p).wait_send()
        push(tx.at[p], back.at[me], b_s.at[p], b_r.at[me], p).wait_send()
        push(etot.at[p], rx2.at[me], e_s.at[p], e_r.at[me], p).wait_send()
        push(tx2.at[p], back2.at[me], c_s.at[p], c_r.at[me], p).wait_send()
        push(gl, gp.at[me], p_s.at[p], p_r.at[me], p).wait_send()
        for group in range(groups):
            push(
                wgs.at[group, p], rwg.at[group, me], t_s.at[group, p], t_r.at[group, me], p
            ).wait_send()
        return carry

    lax.fori_loop(1, n, sent, 0)
    for store in stores:
        store.wait()
    owned_swap.wait()
    wout[partner] = rfin[...]


def hand_on(*refs):
    copies = [pltpu.make_async_copy(refs[i], refs[4 + i], refs[8].at[i]) for i in range(4)]
    for copy in copies:
        copy.start()
    for copy in copies:
        copy.wait()


def fused(n, queries, keys, values, feature_weight, norm_gain, doc_bounds, out_grad):
    tokens, features = queries.shape
    heads = features // HS
    blocks = tokens // BLK
    width = HS // n
    deep = feature_weight.shape[1]
    rows_each = heads * HS // n
    slab_rows = heads * width
    groups = 2
    turned = jnp.swapaxes(feature_weight, 1, 2).reshape(2, slab_rows, deep)
    wx = jnp.concatenate([turned, turned], axis=2)
    factor = float((n * tokens) ** -0.5)
    bf, f32 = jnp.bfloat16, jnp.float32
    vm = pltpu.VMEM
    per = (heads, tokens, HS)
    slabs = (n, rows_each, HS)
    whole = vm((tokens, features), bf)
    scratch = [whole] * 8 + [
        vm((heads, HS), f32), vm((slab_rows, HS), bf), vm((slab_rows, HS), bf),
        vm((n, slab_rows, HS), bf), vm((heads, HS, HS), bf),
        vm((blocks, heads, HS, HS), f32),
        vm(slabs, bf), vm(slabs, bf), vm(slabs, bf), vm(slabs, bf),
        vm(per, bf), vm(per, bf), vm(per, bf),
        vm((heads, HS, blocks * HS), bf), vm(per, bf), vm((blocks, heads, HS, HS), f32),
        vm(slabs, bf), vm(slabs, bf), vm(slabs, bf), vm(slabs, bf),
        vm(per, bf), vm(per, bf), vm(per, f32), vm(per, f32),
        vm((heads, HS, HS), f32),
        vm((groups, n, slab_rows // groups, HS), bf), vm((groups, n, slab_rows // groups, HS), bf),
        vm((heads, HS), f32), vm((n, heads, HS), f32),
        vm((slab_rows, HS), f32), vm((slab_rows, HS), f32),
    ]
    dma = pltpu.SemaphoreType.DMA
    sems = [dma, dma] + [dma((n,))] * 12 + [dma((groups, n))] * 2 + [dma, dma, dma((8,))]
    flat = jax.ShapeDtypeStruct((tokens, features), bf)
    in_vmem = pl.BlockSpec(memory_space=vm)
    anywhere = pl.BlockSpec(memory_space=pl.ANY)
    mixed, qgrad, kgrad, vgrad, wout, gout = pl.pallas_call(
        functools.partial(layer_kernel, n, heads, blocks, doc_bounds.shape[0], factor),
        out_shape=(
            flat, flat, flat, flat,
            jax.ShapeDtypeStruct((2, slab_rows, HS), f32),
            jax.ShapeDtypeStruct((heads, HS), f32),
        ),
        in_specs=[pl.BlockSpec(memory_space=pltpu.SMEM)] + [anywhere] * 4 + [in_vmem] * 2,
        out_specs=(anywhere,) * 4 + (in_vmem,) * 2,
        scratch_shapes=scratch + sems,
        compiler_params=pltpu.CompilerParams(
            collective_id=0, has_side_effects=True, vmem_limit_bytes=52 * 2**20
        ),
        cost_estimate=pl.CostEstimate(
            flops=36 * tokens * features * HS, bytes_accessed=16 * tokens * features,
            transcendentals=0,
        ),
        name="layer",
    )(doc_bounds, queries, keys, values, out_grad, norm_gain, wx)
    mixed, qgrad, kgrad, vgrad = pl.pallas_call(
        hand_on,
        out_shape=(flat,) * 4,
        in_specs=[anywhere] * 4,
        out_specs=(anywhere,) * 4,
        scratch_shapes=[dma((4,))],
        compiler_params=pltpu.CompilerParams(vmem_limit_bytes=62 * 2**20),
        name="hand_on",
    )(mixed, qgrad, kgrad, vgrad)
    owned = wout.reshape(2 * heads, width, HS)
    owned = lax.dynamic_slice_in_dim(owned, lax.axis_index("fsdp") * deep, deep, 2)
    return mixed, qgrad, kgrad, vgrad, jnp.swapaxes(owned, 1, 2), gout


def local(*args):
    n = lax.axis_size("seq")
    heads = args[0].shape[1] // HS
    width = HS // n
    if lax.axis_size("fsdp") == 2 and width == 8 and n % heads == 0 and heads % 4 == 0:
        return fused(n, *args)
    return plain(*args)


def solution(mesh):
    placed = (
        P("seq", "fsdp"),
        P("seq", "fsdp"),
        P("seq", "fsdp"),
        P(None, "fsdp", "seq"),
        P("fsdp", None),
        P(),
        P("seq", "fsdp"),
    )
    return jax.shard_map(
        local,
        mesh=mesh,
        in_specs=placed,
        out_specs=(
            P("seq", "fsdp"),
            P("seq", "fsdp"),
            P("seq", "fsdp"),
            P("seq", "fsdp"),
            P(None, "fsdp", "seq"),
            P("fsdp", None),
        ),
        check_vma=False,
    )
```

```python
import functools

import jax
import jax.numpy as jnp
from jax import lax
from jax.experimental import pallas as pl
from jax.experimental.pallas import tpu as pltpu
from jax.sharding import PartitionSpec as P

HS = 128
BLK = 128


epsilon = 1.0


def carried_in(shard, axis, join, neutral, backward):
    count = lax.axis_size(axis)
    place = lax.axis_index(axis)
    ahead = count - 1 - place if backward else place
    gathered = jax.tree.map(
        lambda a, kind: lax.all_gather(a.astype(kind), axis), shard, (jnp.bfloat16, jnp.bfloat16)
    )
    state = jax.tree.map(lambda a, e: jnp.zeros_like(a) + jnp.asarray(e, a.dtype), shard, neutral)

    def one(hop, state):
        source = count - 1 - hop if backward else hop
        return join(
            state,
            jax.tree.map(
                lambda a, own: lax.dynamic_index_in_dim(a, source, 0, False).astype(own.dtype),
                gathered,
                shard,
            ),
        )

    return lax.fori_loop(0, ahead, one, state)


def chain_states(earlier, later):
    early_state, early_flag = earlier
    late_state, late_flag = later
    return (
        jnp.where(late_flag > 0.0, late_state, early_state + late_state),
        jnp.maximum(early_flag, late_flag),
    )


def project(rows, weight):
    return jnp.einsum("bthd,hde->bthe", rows, weight, preferred_element_type=jnp.float32).astype(
        jnp.bfloat16
    )


def plain(queries, keys, values, feature_weight, norm_gain, doc_bounds, out_grad):
    rows_full = lax.all_gather(feature_weight, "seq", axis=2, tiled=True)
    weight_local = lax.all_to_all(rows_full, "fsdp", split_axis=0, concat_axis=1, tiled=True)
    head_count = weight_local.shape[0]
    tokens_here = queries.shape[0]
    block_count = tokens_here // BLK
    block_shape = (block_count, BLK, head_count, HS)
    query_blocks = queries.reshape(block_shape)
    key_blocks = keys.reshape(block_shape)
    value_blocks = values.reshape(block_shape)
    qfeat = project(query_blocks, weight_local)
    kfeat = project(key_blocks, weight_local)
    first_block = lax.axis_index("seq") * block_count
    block_ids = first_block + jnp.arange(block_count, dtype=jnp.int32)
    starts = doc_bounds[:, 0]
    starts_here = jnp.any(starts[None, :] == block_ids[:, None], axis=1)
    opened = jnp.cumsum(starts_here.astype(jnp.int32))
    reach_left = opened == 0
    reach_right = opened[-1] - opened == 0
    has_start = jnp.any(starts_here).astype(jnp.float32)
    updates = jnp.einsum("bthe,bthf->bhef", kfeat, value_blocks, preferred_element_type=jnp.float32)
    zero_state = jnp.zeros(updates.shape[1:], jnp.float32)
    zero_flag = jnp.zeros((), jnp.float32)
    running = zero_state
    prefix_list = []
    for position in range(block_count):
        held = jnp.where(starts_here[position], zero_state, running)
        prefix_list.append(held)
        running = held + updates[position]
    entering, _ = carried_in(
        (running, has_start), "seq", chain_states, (zero_state, zero_flag), False
    )
    states = jnp.stack(prefix_list) + jnp.where(
        reach_left[:, None, None, None], entering[None], 0.0
    )
    state_half = states.astype(jnp.bfloat16)
    causal = jnp.arange(BLK)[:, None] >= jnp.arange(BLK)[None, :]
    scores = jnp.einsum("bthe,bshe->bhts", qfeat, kfeat, preferred_element_type=jnp.float32)
    prob_half = jnp.where(causal, scores, 0.0).astype(jnp.bfloat16)
    mixed_f = jnp.einsum("bthe,bhef->bthf", qfeat, state_half, preferred_element_type=jnp.float32)
    mixed_f = mixed_f + jnp.einsum(
        "bhts,bshf->bthf", prob_half, value_blocks, preferred_element_type=jnp.float32
    )
    gains = norm_gain.astype(jnp.float32)
    inverse = lax.rsqrt(jnp.mean(mixed_f * mixed_f, axis=-1, keepdims=True) + epsilon)
    mixed = (mixed_f * inverse * gains).astype(jnp.bfloat16)
    grad_y = out_grad.reshape(block_shape).astype(jnp.float32)
    scaled = grad_y * gains
    grad_mix = inverse * (
        scaled - mixed_f * inverse * inverse * jnp.mean(scaled * mixed_f, axis=-1, keepdims=True)
    )
    grad_half = grad_mix.astype(jnp.bfloat16)
    gain_part = jnp.sum(grad_y * mixed_f * inverse, axis=(0, 1))
    state_grads = jnp.einsum(
        "bthe,bthf->bhef", qfeat, grad_half, preferred_element_type=jnp.float32
    )
    running = zero_state
    suffix_list = [zero_state] * block_count
    for position in reversed(range(block_count)):
        suffix_list[position] = running
        running = jnp.where(starts_here[position], zero_state, running + state_grads[position])
    leaving, _ = carried_in(
        (running, has_start), "seq", chain_states, (zero_state, zero_flag), True
    )
    suffix = jnp.stack(suffix_list) + jnp.where(
        reach_right[:, None, None, None], leaving[None], 0.0
    )
    suffix_half = suffix.astype(jnp.bfloat16)
    dot_grads = jnp.einsum(
        "bthf,bshf->bhts", grad_half, value_blocks, preferred_element_type=jnp.float32
    )
    dot_half = jnp.where(causal, dot_grads, 0.0).astype(jnp.bfloat16)
    qfeat_grad = jnp.einsum(
        "bthf,bhef->bthe", grad_half, state_half, preferred_element_type=jnp.float32
    )
    qfeat_grad = (
        qfeat_grad
        + jnp.einsum("bhts,bshe->bthe", dot_half, kfeat, preferred_element_type=jnp.float32)
    ).astype(jnp.bfloat16)
    kfeat_grad = jnp.einsum(
        "bshf,bhef->bshe", value_blocks, suffix_half, preferred_element_type=jnp.float32
    )
    kfeat_grad = (
        kfeat_grad
        + jnp.einsum("bhts,bthe->bshe", dot_half, qfeat, preferred_element_type=jnp.float32)
    ).astype(jnp.bfloat16)
    value_grad = jnp.einsum(
        "bshe,bhef->bshf", kfeat, suffix_half, preferred_element_type=jnp.float32
    )
    value_grad = (
        value_grad
        + jnp.einsum("bhts,bthf->bshf", prob_half, grad_half, preferred_element_type=jnp.float32)
    ).astype(jnp.bfloat16)
    query_grad = jnp.einsum(
        "bthe,hde->bthd", qfeat_grad, weight_local, preferred_element_type=jnp.float32
    ).astype(jnp.bfloat16)
    key_grad = jnp.einsum(
        "bthe,hde->bthd", kfeat_grad, weight_local, preferred_element_type=jnp.float32
    ).astype(jnp.bfloat16)
    weight_part = jnp.einsum(
        "bthd,bthe->hde", query_blocks, qfeat_grad, preferred_element_type=jnp.float32
    )
    weight_part = weight_part + jnp.einsum(
        "bthd,bthe->hde", key_blocks, kfeat_grad, preferred_element_type=jnp.float32
    )
    weight_sum, gain_sum = lax.psum((weight_part, gain_part), "seq")
    column_width = weight_sum.shape[2] // lax.axis_size("seq")
    weight_columns = lax.dynamic_slice_in_dim(
        weight_sum, lax.axis_index("seq") * column_width, column_width, 2
    )
    owned_grad = lax.all_to_all(weight_columns, "fsdp", split_axis=1, concat_axis=0, tiled=True)
    factor = (lax.axis_size("seq") * tokens_here) ** (-0.5)
    flat_shape = (tokens_here, head_count * HS)
    return (
        mixed.reshape(flat_shape),
        query_grad.reshape(flat_shape),
        key_grad.reshape(flat_shape),
        value_grad.reshape(flat_shape),
        owned_grad * factor,
        gain_sum * factor,
    )

MESH = pl.DeviceIdType.MESH


def nn(a, b):
    return lax.dot_general(a, b, (((1,), (0,)), ((), ())), preferred_element_type=jnp.float32)


def nt(a, b):
    return lax.dot_general(a, b, (((1,), (1,)), ((), ())), preferred_element_type=jnp.float32)


def tn(a, b):
    return lax.dot_general(a, b, (((0,), (0,)), ((), ())), preferred_element_type=jnp.float32)


def layer_kernel(
    n, heads, blocks, docs, factor,
    bounds, q_in, k_in, v_in, og_in, gain, wx,
    mixed_out, qgrad_out, kgrad_out, vgrad_out, wout, gout,
    q, k, v, og, mixed, qgrad, kgrad, vgrad,
    gain_f, wslab, wpart, gw, wt, mloc, mtot, rx, tx, back,
    qf, kf, prob, sh, dh, eloc, etot, rx2, tx2, back2,
    dotq, dqf, dkp, vgp, wgt, wgs, rwg, gl, gp, fin, rfin,
    w_s, w_r, g_s, g_r, h_s, m_s, m_r, b_s, b_r, e_s, e_r, c_s, c_r, p_s, p_r, t_s, t_r, f_s, f_r, io,
):
    me = lax.axis_index("seq")
    mine = lax.axis_index("fsdp")
    partner = 1 - mine
    per_head = n // heads
    slab = HS // per_head
    width = HS // n
    groups = t_s.shape[0]
    group_rows = heads * width // groups

    barrier = pltpu.get_barrier_semaphore()

    def greet(step, carry):
        pl.semaphore_signal(
            barrier, inc=1, device_id={"seq": lax.rem(me + step, n)}, device_id_type=MESH
        )
        return carry

    lax.fori_loop(1, n, greet, 0)
    pl.semaphore_signal(barrier, inc=1, device_id={"fsdp": partner}, device_id_type=MESH)

    loads = [
        pltpu.make_async_copy(a, b, io.at[i])
        for i, (a, b) in enumerate([(k_in, k), (v_in, v), (q_in, q), (og_in, og)])
    ]
    for load in loads:
        load.start()
    stores = [
        pltpu.make_async_copy(a, b, io.at[4 + i])
        for i, (a, b) in enumerate(
            [(mixed, mixed_out), (qgrad, qgrad_out), (kgrad, kgrad_out), (vgrad, vgrad_out)]
        )
    ]

    def push(src, dst, send, recv, p):
        return pltpu.make_async_remote_copy(
            src_ref=src, dst_ref=dst, send_sem=send, recv_sem=recv,
            device_id={"seq": p}, device_id_type=MESH,
        )

    def opens_in(first, count):
        found = jnp.float32(0.0)
        for i in range(docs):
            s = bounds[i, 0]
            found = jnp.where(jnp.logical_and(s >= first, s < first + count), 1.0, found)
        return found

    def columns(h):
        return pl.ds(pl.multiple_of(h * HS, HS), HS)

    def rows(b):
        return pl.ds(b * BLK, BLK)

    cont = [1.0 - opens_in(me * blocks + b, 1) for b in range(blocks)]
    reach_left = []
    value = jnp.float32(1.0)
    for b in range(blocks):
        value = value * cont[b]
        reach_left.append(value)
    reach_right = [None] * blocks
    value = jnp.float32(1.0)
    for b in reversed(range(blocks)):
        reach_right[b] = value
        value = value * cont[b]

    gain_f[...] = gain[...].astype(jnp.float32)

    def outer_products(quad, carry):
        heads_here = [4 * quad + j for j in range(4)]
        terms = [
            [tn(k[rows(b), columns(h)], v[rows(b), columns(h)]) for b in range(blocks)]
            for h in heads_here
        ]
        for h, term in zip(heads_here, terms):
            run = jnp.zeros((HS, HS), jnp.float32)
            for b in range(blocks):
                held = run * cont[b]
                mloc[b, h] = held
                run = held + term[b]
            mtot[pl.ds(h * per_head, per_head)] = run.reshape(per_head, slab, HS).astype(
                jnp.bfloat16
            )
        return carry

    loads[0].wait()
    loads[1].wait()
    lax.fori_loop(0, heads // 4, outer_products, 0)
    pl.semaphore_wait(barrier, n)

    weight_swap = pltpu.make_async_remote_copy(
        src_ref=wx.at[partner], dst_ref=wpart, send_sem=w_s, recv_sem=w_r,
        device_id={"fsdp": partner}, device_id_type=MESH,
    )
    weight_swap.start()

    def send_totals(step, carry):
        p = lax.rem(me + step, n)
        push(mtot.at[p], rx.at[me], m_s.at[p], m_r.at[me], p).start()
        return carry

    lax.fori_loop(1, n, send_totals, 0)
    weight_swap.wait()
    lane = lax.broadcasted_iota(jnp.int32, wslab.shape, 1)
    own_lane = (lane // (HS // 2)) == mine
    wslab[...] = jnp.where(
        own_lane, wx[mine].astype(jnp.float32), wpart[...].astype(jnp.float32)
    ).astype(jnp.bfloat16)

    def send_weights(step, carry):
        p = lax.rem(me + 2 * step, n)
        push(wslab, gw.at[me], g_s.at[p], g_r.at[me], p).start()
        return carry

    sibling = me + 1 - 2 * lax.rem(me, 2)
    lax.fori_loop(1, n // 2, send_weights, 0)
    gw[me] = wslab[...]
    push(gw.at[me], gw.at[me], h_s.at[me], g_r.at[me], sibling).start()

    def forward_weights(step, carry):
        p = lax.rem(me + n - 2 * step, n)
        push(wslab, gw.at[p], g_s.at[p], g_r.at[p], p).wait_recv()
        push(gw.at[p], gw.at[p], h_s.at[p], g_r.at[p], sibling).start()
        return carry

    lax.fori_loop(1, n // 2, forward_weights, 0)

    def scan(total, arrived, parts, entered, in_s, in_r, out_s, out_r, backward):
        arrived[me] = total[me]

        def one(step, state):
            p = n - 1 - step if backward else step

            @pl.when(p != me)
            def _():
                push(total.at[p], arrived.at[p], in_s.at[p], in_r.at[p], p).wait_recv()

            parts[p] = state.astype(jnp.bfloat16)

            @pl.when(p != me)
            def _():
                push(parts.at[p], entered.at[me], out_s.at[p], out_r.at[me], p).start()

            keep = 1.0 - opens_in(p * blocks, blocks)
            return state * keep + arrived[p].astype(jnp.float32)

        lax.fori_loop(0, n, one, jnp.zeros((slab, HS), jnp.float32))
        entered[me] = parts[me]

    def entering(pair, parts, entered, out_s, out_r):
        for j in range(2 * per_head):
            p = pair * 2 * per_head + j

            @pl.when(p != me)
            def _():
                push(parts.at[p], entered.at[p], out_s.at[p], out_r.at[p], p).wait_recv()

        both = entered[pl.ds(pair * 2 * per_head, 2 * per_head)].astype(jnp.float32)
        return [both[:per_head].reshape(HS, HS), both[per_head:].reshape(HS, HS)]

    scan(mtot, rx, tx, back, m_s, m_r, b_s, b_r, False)

    def await_weights(step, carry):
        p = lax.rem(sibling + n - 2 * step, n)
        push(gw.at[p], gw.at[p], h_s.at[p], g_r.at[p], sibling).wait_recv()
        return carry

    lax.fori_loop(0, n // 2, await_weights, 0)
    causal = lax.broadcasted_iota(jnp.int32, (BLK, BLK), 0) >= lax.broadcasted_iota(
        jnp.int32, (BLK, BLK), 1
    )

    def project_pair(pair, carry):
        both = gw[:, pl.ds(pl.multiple_of(pair * 2 * width, 2 * width), 2 * width), :]
        both = both.astype(jnp.float32)
        features = []
        for j in range(2):
            h = 2 * pair + j
            weight = both[:, j * width : (j + 1) * width, :].reshape(HS, HS).astype(jnp.bfloat16)
            wt[h] = weight
            qh = nt(q[:, columns(h)], weight).astype(jnp.bfloat16)
            kh = nt(k[:, columns(h)], weight).astype(jnp.bfloat16)
            qf[h] = qh
            kf[h] = kh
            features.append((h, qh, kh))
        for h, qh, kh in features:
            for b in range(blocks):
                at = slice(b * BLK, (b + 1) * BLK)
                prob[h, rows(b), :] = jnp.where(causal, nt(qh[at], kh[at]), 0.0).astype(
                    jnp.bfloat16
                )
        return carry

    loads[2].wait()
    lax.fori_loop(0, heads // 2, project_pair, 0)
    loads[3].wait()

    def forward(pair, carry):
        enters = entering(pair, tx, back, b_s, b_r)
        heads_here = (2 * pair, 2 * pair + 1)
        states = []
        for h, enter in zip(heads_here, enters):
            memory = jnp.concatenate(
                [
                    (mloc[b, h] + reach_left[b] * enter).astype(jnp.bfloat16)
                    for b in range(blocks)
                ],
                axis=1,
            )
            states.append(nn(wt[h], memory).astype(jnp.bfloat16))
        outs = []
        for h, state in zip(heads_here, states):
            sh[h] = state
            for b in range(blocks):
                both = jnp.concatenate([qf[h, rows(b), :], prob[h, rows(b), :]], axis=1)
                held = jnp.concatenate(
                    [state[:, b * HS : (b + 1) * HS], v[rows(b), columns(h)]], axis=0
                )
                outs.append(nn(both, held))
        terms = []
        for i, h in enumerate(heads_here):
            g = gain_f[pl.ds(h, 1), :]
            gain_sum = jnp.zeros((1, HS), jnp.float32)
            for b in range(blocks):
                o = outs[i * blocks + b]
                r = lax.rsqrt(jnp.mean(o * o, axis=-1, keepdims=True) + epsilon)
                normed = o * r
                mixed[rows(b), columns(h)] = (normed * g).astype(jnp.bfloat16)
                gy = og[rows(b), columns(h)].astype(jnp.float32)
                scaled = gy * g
                inner = jnp.mean(scaled * o, axis=-1, keepdims=True)
                d = (r * (scaled - normed * (r * inner))).astype(jnp.bfloat16)
                dh[h, rows(b), :] = d
                gain_sum = gain_sum + jnp.sum(gy * normed, axis=0, keepdims=True)
                terms.append(tn(qf[h, rows(b), :], d))
            gl[pl.ds(h, 1), :] = gain_sum
        for i, h in enumerate(heads_here):
            run = jnp.zeros((HS, HS), jnp.float32)
            for b in reversed(range(blocks)):
                eloc[b, h] = run
                run = (run + terms[i * blocks + b]) * cont[b]
            etot[pl.ds(h * per_head, per_head)] = run.reshape(per_head, slab, HS).astype(
                jnp.bfloat16
            )
        for j in range(2 * per_head):
            p = pair * 2 * per_head + j

            @pl.when(p != me)
            def _():
                push(etot.at[p], rx2.at[me], e_s.at[p], e_r.at[me], p).start()

        return carry

    lax.fori_loop(0, heads // 2, forward, 0)
    stores[0].start()

    def send_gain(step, carry):
        p = lax.rem(me + step, n)
        push(gl, gp.at[me], p_s.at[p], p_r.at[me], p).start()
        return carry

    lax.fori_loop(1, n, send_gain, 0)
    gp[me] = gl[...]

    def query_side(quad, carry):
        for h in [4 * quad + j for j in range(4)]:
            scores = []
            for b in range(blocks):
                score = nt(dh[h, rows(b), :], v[rows(b), columns(h)])
                scores.append(jnp.where(causal, score, 0.0).astype(jnp.bfloat16))
            for b in range(blocks):
                dotq[h, rows(b), :] = scores[b]
                dqf[h, rows(b), :] = (
                    nt(dh[h, rows(b), :], sh[h, :, rows(b)]) + nn(scores[b], kf[h, rows(b), :])
                ).astype(jnp.bfloat16)
        return carry

    lax.fori_loop(0, heads // 4, query_side, 0)
    scan(etot, rx2, tx2, back2, e_s, e_r, c_s, c_r, True)

    def local_terms(quad, carry):
        for h in [4 * quad + j for j in range(4)]:
            grads = dqf[h]
            qgrad[:, columns(h)] = nn(grads, wt[h]).astype(jnp.bfloat16)
            wgt[h] = tn(grads, q[:, columns(h)])
            for b in range(blocks):
                dkp[h, rows(b), :] = tn(dotq[h, rows(b), :], qf[h, rows(b), :])
                vgp[h, rows(b), :] = tn(prob[h, rows(b), :], dh[h, rows(b), :])
        return carry

    lax.fori_loop(0, heads // 4, local_terms, 0)
    stores[1].start()

    def key_pair_grads(pair):
        enters = entering(pair, tx2, back2, c_s, c_r)
        heads_here = (2 * pair, 2 * pair + 1)
        grads = []
        for h, enter in zip(heads_here, enters):
            parts = []
            for b in range(blocks):
                memory = (eloc[b, h] + reach_right[b] * enter).astype(jnp.bfloat16)
                vb = v[rows(b), columns(h)]
                parts.append((nt(vb, memory) + dkp[h, rows(b), :]).astype(jnp.bfloat16))
                vgrad[rows(b), columns(h)] = (
                    nn(kf[h, rows(b), :], memory) + vgp[h, rows(b), :]
                ).astype(jnp.bfloat16)
            grads.append(jnp.concatenate(parts, axis=0))
        totals = []
        for h, grad in zip(heads_here, grads):
            kgrad[:, columns(h)] = nn(grad, wt[h]).astype(jnp.bfloat16)
            totals.append((wgt[h] + tn(grad, k[:, columns(h)])).reshape(n, width, HS))
        return jnp.concatenate(totals, axis=1)

    pairs = heads // 2 // groups

    def key_group(group, carry):
        def key_pair(i, inner):
            pair = group * pairs + i
            both = key_pair_grads(pair)
            wgs[group, :, pl.ds(pl.multiple_of(i * 2 * width, 2 * width), 2 * width), :] = (
                both.astype(jnp.bfloat16)
            )
            return inner

        lax.fori_loop(0, pairs, key_pair, 0)

        def send_terms(step, inner):
            p = lax.rem(me + step, n)
            push(
                wgs.at[group, p], rwg.at[group, me], t_s.at[group, p], t_r.at[group, me], p
            ).start()
            return inner

        lax.fori_loop(1, n, send_terms, 0)
        rwg[group, me] = wgs[group, me]
        return carry

    lax.fori_loop(0, groups, key_group, 0)
    stores[2].start()
    stores[3].start()

    def add_gain(step, carry):
        p = lax.rem(me + n - step, n)
        push(gl, gp.at[p], p_s.at[p], p_r.at[p], p).wait_recv()
        return carry

    lax.fori_loop(1, n, add_gain, 0)
    gout[...] = jnp.sum(gp[...], axis=0) * factor

    for group in range(groups):

        def arrive(step, total):
            p = lax.rem(me + n - step, n)
            push(
                wgs.at[group, p], rwg.at[group, p], t_s.at[group, p], t_r.at[group, p], p
            ).wait_recv()
            return total + rwg[group, p].astype(jnp.float32)

        total = lax.fori_loop(1, n, arrive, rwg[group, me].astype(jnp.float32))
        fin[pl.ds(group * group_rows, group_rows), :] = total * factor

    owned_swap = pltpu.make_async_remote_copy(
        src_ref=fin, dst_ref=rfin, send_sem=f_s, recv_sem=f_r,
        device_id={"fsdp": partner}, device_id_type=MESH,
    )
    owned_swap.start()
    wout[mine] = fin[...]

    def sent(step, carry):
        p = lax.rem(me + step, n)
        push(mtot.at[p], rx.at[me], m_s.at[p], m_r.at[me], p).wait_send()
        push(tx.at[p], back.at[me], b_s.at[p], b_r.at[me], p).wait_send()
        push(etot.at[p], rx2.at[me], e_s.at[p], e_r.at[me], p).wait_send()
        push(tx2.at[p], back2.at[me], c_s.at[p], c_r.at[me], p).wait_send()
        push(gl, gp.at[me], p_s.at[p], p_r.at[me], p).wait_send()
        for group in range(groups):
            push(
                wgs.at[group, p], rwg.at[group, me], t_s.at[group, p], t_r.at[group, me], p
            ).wait_send()
        return carry

    lax.fori_loop(1, n, sent, 0)

    def sent_weights(step, carry):
        p = lax.rem(me + 2 * step, n)

        @pl.when(step > 0)
        def _():
            push(wslab, gw.at[me], g_s.at[p], g_r.at[me], p).wait_send()

        push(gw.at[p], gw.at[p], h_s.at[p], g_r.at[p], sibling).wait_send()
        return carry

    lax.fori_loop(0, n // 2, sent_weights, 0)
    for store in stores:
        store.wait()
    owned_swap.wait()
    wout[partner] = rfin[...]


def hand_on(mixed, qgrad, kgrad, vgrad, gains, *refs):
    outs, held, sems = refs[:5], refs[5], refs[6]
    half = mixed.shape[0] // 2
    loads, stores = [], []
    for i, array in enumerate((mixed, qgrad, kgrad, vgrad)):
        for j in range(2):
            at = pl.ds(j * half, half)
            stop = held.at[i, at, :]
            loads.append(pltpu.make_async_copy(array.at[at, :], stop, sems.at[0, i, j]))
            stores.append(pltpu.make_async_copy(stop, outs[i].at[at, :], sems.at[1, i, j]))
    for load in loads:
        load.start()
    outs[4][...] = gains[...]
    for load, store in zip(loads, stores):
        load.wait()
        store.start()
    for store in stores:
        store.wait()


def fused(n, queries, keys, values, feature_weight, norm_gain, doc_bounds, out_grad):
    tokens, features = queries.shape
    heads = features // HS
    blocks = tokens // BLK
    width = HS // n
    deep = feature_weight.shape[1]
    rows_each = heads * HS // n
    slab_rows = heads * width
    groups = 2
    turned = jnp.swapaxes(feature_weight, 1, 2).reshape(2, slab_rows, deep)
    wx = jnp.concatenate([turned, turned], axis=2)
    factor = float((n * tokens) ** -0.5)
    bf, f32 = jnp.bfloat16, jnp.float32
    vm = pltpu.VMEM
    per = (heads, tokens, HS)
    slabs = (n, rows_each, HS)
    whole = vm((tokens, features), bf)
    scratch = [whole] * 8 + [
        vm((heads, HS), f32), vm((slab_rows, HS), bf), vm((slab_rows, HS), bf),
        vm((n, slab_rows, HS), bf), vm((heads, HS, HS), bf),
        vm((blocks, heads, HS, HS), f32),
        vm(slabs, bf), vm(slabs, bf), vm(slabs, bf), vm(slabs, bf),
        vm(per, bf), vm(per, bf), vm(per, bf),
        vm((heads, HS, blocks * HS), bf), vm(per, bf), vm((blocks, heads, HS, HS), f32),
        vm(slabs, bf), vm(slabs, bf), vm(slabs, bf), vm(slabs, bf),
        vm(per, bf), vm(per, bf), vm(per, f32), vm(per, f32),
        vm((heads, HS, HS), f32),
        vm((groups, n, slab_rows // groups, HS), bf), vm((groups, n, slab_rows // groups, HS), bf),
        vm((heads, HS), f32), vm((n, heads, HS), f32),
        vm((slab_rows, HS), f32), vm((slab_rows, HS), f32),
    ]
    dma = pltpu.SemaphoreType.DMA
    sems = [dma, dma] + [dma((n,))] * 13 + [dma((groups, n))] * 2 + [dma, dma, dma((8,))]
    flat = jax.ShapeDtypeStruct((tokens, features), bf)
    in_vmem = pl.BlockSpec(memory_space=vm)
    anywhere = pl.BlockSpec(memory_space=pl.ANY)
    mixed, qgrad, kgrad, vgrad, wout, gout = pl.pallas_call(
        functools.partial(layer_kernel, n, heads, blocks, doc_bounds.shape[0], factor),
        out_shape=(
            flat, flat, flat, flat,
            jax.ShapeDtypeStruct((2, slab_rows, HS), f32),
            jax.ShapeDtypeStruct((heads, HS), f32),
        ),
        in_specs=[pl.BlockSpec(memory_space=pltpu.SMEM)] + [anywhere] * 4 + [in_vmem] * 2,
        out_specs=(anywhere,) * 4 + (in_vmem,) * 2,
        scratch_shapes=scratch + sems,
        compiler_params=pltpu.CompilerParams(
            collective_id=0, has_side_effects=True, vmem_limit_bytes=58 * 2**20
        ),
        cost_estimate=pl.CostEstimate(
            flops=36 * tokens * features * HS, bytes_accessed=16 * tokens * features,
            transcendentals=0,
        ),
        name="layer",
    )(doc_bounds, queries, keys, values, out_grad, norm_gain, wx)
    mixed, qgrad, kgrad, vgrad, gout = pl.pallas_call(
        hand_on,
        out_shape=(flat,) * 4 + (jax.ShapeDtypeStruct((heads, HS), f32),),
        in_specs=[anywhere] * 4 + [in_vmem],
        out_specs=(anywhere,) * 4 + (in_vmem,),
        scratch_shapes=[vm((4, tokens, features), bf), dma((2, 4, 2))],
        compiler_params=pltpu.CompilerParams(vmem_limit_bytes=60 * 2**20),
        name="hand_on",
    )(mixed, qgrad, kgrad, vgrad, gout)
    owned = wout.reshape(2 * heads, width, HS)
    owned = lax.dynamic_slice_in_dim(owned, lax.axis_index("fsdp") * deep, deep, 2)
    return mixed, qgrad, kgrad, vgrad, jnp.swapaxes(owned, 1, 2), gout


def local(*args):
    n = lax.axis_size("seq")
    heads = args[0].shape[1] // HS
    width = HS // n
    if lax.axis_size("fsdp") == 2 and width == 8 and n % heads == 0 and heads % 4 == 0:
        return fused(n, *args)
    return plain(*args)


def solution(mesh):
    placed = (
        P("seq", "fsdp"),
        P("seq", "fsdp"),
        P("seq", "fsdp"),
        P(None, "fsdp", "seq"),
        P("fsdp", None),
        P(),
        P("seq", "fsdp"),
    )
    return jax.shard_map(
        local,
        mesh=mesh,
        in_specs=placed,
        out_specs=(
            P("seq", "fsdp"),
            P("seq", "fsdp"),
            P("seq", "fsdp"),
            P("seq", "fsdp"),
            P(None, "fsdp", "seq"),
            P("fsdp", None),
        ),
        check_vma=False,
    )
```
